32 devices in a mesh: scen: 2 (over y), tm: 8 (over z, x), xfmr: 2 (over core).
Axes of the slice: x: 2, y: 2, z: 4, core: 2. Of those that a mesh axis runs over, the one named last changes fastest.
Arguments:
- voltages: bfloat16 [8, 512, 8192], P('scen', 'tm', 'xfmr'), parts along dimension 0, may hold values from -6 to 6
- coupling: bfloat16 [96, 4, 128, 128], P('xfmr'), may hold values from -0.25 to 0.25
- pattern: int32 [96, 4], P('xfmr'), may hold values from 0 to 63
- substation: int32 [12288], P('xfmr'), may hold values from 0 to 255
- time_const: float32 [256, 2], replicated, may hold values from 30 to 2048
- amplitude: float32 [256, 2], replicated, may hold values from 0.5 to 2
Outputs:
- hot_spot: bfloat16 [8, 512, 12288], P('scen', 'tm', 'xfmr'), parts along dimension 0
The draws below stay inside these ranges and needn't reach their ends.
There are 2 independent parts, one for each index of `scen`. The reference program is written for one: setup_inputs(seed, part) draws one part's arguments, and reference() takes and returns one part's arrays. A program takes and returns all parts, laid end to end along the dimension named above; an argument that names none is the same for every part. Nothing has to cross between parts.
All inputs are finite; a program needn't handle non-finite values.
Results may differ from the reference program's by a relative error of at most 0.002.
Values may be sent and summed in bfloat16 or wider, within the bound.
A program may use at most 128 MiB of HBM per device.

```python
import math
import jax
import jax.numpy as jnp
from jax import lax

SCEN = 4
LINES = 8192
XF = 12288
BL = 128
BX = 128
NNZ = 4
GROUPS = 256
R = 2
TIME = 512


def touch_ends(drawn, stream_key, smallest, top_value):
    longest = drawn.shape.index(max(drawn.shape))
    spots = []
    for shift in (0, 1):
        where = [jax.random.randint(jax.random.fold_in(stream_key, axis), (), 0, length) for axis, length in enumerate(drawn.shape)]
        where[longest] = (where[longest] + shift) % drawn.shape[longest]
        spots.append(tuple(where))
    return drawn.at[spots[0]].set(smallest).at[spots[1]].set(top_value)


def levels(own_key, extent, shards, low, top_value):
    factor_of, own = 1.0, jax.random.fold_in(own_key, 6)
    for dim, parts in shards:
        draws = jnp.exp(jax.random.uniform(jax.random.fold_in(own, dim), (parts,), jnp.float32, low / len(shards), top_value / len(shards)))
        factor_of = factor_of * jnp.repeat(draws, extent[dim] // parts).reshape([-1 if axis == dim else 1 for axis in range(len(extent))])
    return factor_of


def gaussian(stream_key, dims, width, reach, cuts=(), dtype=jnp.bfloat16):
    array = jax.random.normal(stream_key, dims, jnp.float32) * width
    if len(cuts) > 0:
        array = levels(stream_key, dims, cuts, -0.22, 0.18) * array
    return jnp.clip(array, min=-reach, max=reach).astype(dtype)


def setup_inputs(seed: int = 0, part: int = 0) -> dict:
    key_list = jax.random.split(jax.random.key(seed), 7)
    own_keys = jax.random.split(jax.random.fold_in(key_list[6], part), 7)
    return {
        "voltages": gaussian(own_keys[0], (SCEN, TIME, LINES), 1.0, 6.0, ((1, 8), (2, 2))),
        "coupling": gaussian(key_list[1], (XF // BX, NNZ, BL, BX), (NNZ * BL) ** -0.5, 0.25, ((0, 2),)),
        "pattern": touch_ends(jax.random.randint(key_list[2], (XF // BX, NNZ), 0, LINES // BL), jax.random.fold_in(key_list[2], 1), 0, (LINES // BL) - 1).astype(jnp.int32),
        "substation": touch_ends(jax.random.randint(key_list[3], (XF,), 0, GROUPS), jax.random.fold_in(key_list[3], 1), 0, GROUPS - 1).astype(jnp.int32),
        "time_const": jnp.clip(jnp.exp(jax.random.uniform(key_list[4], (GROUPS, R), jnp.float32, math.log(30.0), math.log(2048.0))), 30.0, 2048.0),
        "amplitude": jnp.clip(jnp.exp(jax.random.uniform(key_list[5], (GROUPS, R), jnp.float32, math.log(0.5), math.log(2.0))), 0.5, 2.0),
    }


def reference(voltages, coupling, pattern, substation, time_const, amplitude):
    block_total = XF // BX

    def couple_one(series):
        panels = series.reshape(TIME, LINES // BL, BL)
        total = jnp.zeros((TIME, block_total, BX), jnp.float32)
        for slot_index in range(NNZ):
            picked = panels[:, pattern[:, slot_index], :]
            total = total + jnp.einsum('txl,xlk->txk', picked.astype(jnp.float32), coupling[:, slot_index].astype(jnp.float32))
        return total.reshape(TIME, XF)

    currents = lax.map(couple_one, voltages)
    heating = jnp.abs(currents).astype(jnp.bfloat16).astype(jnp.float32)
    rates = 1.0 / time_const[substation]
    decay = jnp.exp(-rates)
    scales = amplitude[substation] * (1.0 - decay)

    def advance(thermal, heat_now):
        thermal = decay * thermal + heat_now[..., None]
        return thermal, jnp.sum(scales * thermal, axis=-1)

    start = jnp.zeros((SCEN, XF, R), jnp.float32)
    _, readings = lax.scan(advance, start, jnp.swapaxes(heating, 0, 1))
    return jnp.swapaxes(readings, 0, 1).astype(jnp.bfloat16)
```

```python
import functools
import jax
import jax.numpy as jnp
from jax import lax
from jax.experimental import pallas as pl
from jax.experimental.pallas import tpu as pltpu
from jax.sharding import PartitionSpec as P

MESH = pl.DeviceIdType.MESH
CHUNK = 8


def kernel(
    pairs, volt_ref, coup_ref, pat_ref, sub_ref, tc_ref, amp_ref, out_ref,
    vbuf, cbuf, hbuf, grow, fade, ends, peer_ends, chain_in, chain_out, carry, span, once,
    tab, lower, obuf,
    volt_sem, coup_sem, out_sem, gather_send, gather_recv, peer_send, peer_recv, chain_send, chain_recv,
):
    scen, steps, lines = volt_ref.shape
    blocks, depth, width = coup_ref.shape
    rows = scen * steps
    groups = tc_ref.shape[1]
    slots = pat_ref.shape[1]
    panel = depth // slots
    chunks = blocks // CHUNK
    core = lax.axis_index("xfmr")
    me = lax.axis_index("tm")
    pair = me // 2
    odd = me % 2
    partner = me + 1 - 2 * odd
    has_prev = pair > 0
    has_next = pair < pairs - 1

    barrier = pltpu.get_barrier_semaphore()
    pl.semaphore_signal(barrier, inc=1, device_id={"xfmr": 1 - core}, device_id_type=MESH)
    pl.semaphore_signal(barrier, inc=1, device_id={"tm": partner}, device_id_type=MESH)

    @pl.when(has_prev)
    def _():
        pl.semaphore_signal(barrier, inc=1, device_id={"tm": me - 2}, device_id_type=MESH)

    @pl.when(has_next)
    def _():
        pl.semaphore_signal(barrier, inc=1, device_id={"tm": me + 2}, device_id_type=MESH)

    panels = lines // panel

    def local_panel(n):
        return pltpu.make_async_copy(
            volt_ref.at[:, :, pl.ds(pl.multiple_of(n * panel, panel), panel)],
            vbuf.at[core * panels + n],
            volt_sem.at[n],
        )

    def sent_panel(n):
        return pltpu.make_async_remote_copy(
            src_ref=volt_ref.at[:, :, pl.ds(pl.multiple_of(n * panel, panel), panel)],
            dst_ref=vbuf.at[core * panels + n],
            send_sem=gather_send.at[n],
            recv_sem=gather_recv.at[n],
            device_id={"xfmr": 1 - core},
            device_id_type=MESH,
        )

    def start_local(n, _):
        local_panel(n).start()
        return 0

    def start_sent(n, _):
        sent_panel(n).start()
        return 0

    def wait_panels(n, _):
        local_panel(n).wait()
        sent_panel(n).wait()
        return 0

    local_coup = pltpu.make_async_copy(coup_ref, cbuf, coup_sem)
    pl.semaphore_wait(barrier, 2 + has_prev.astype(jnp.int32) + has_next.astype(jnp.int32))
    lax.fori_loop(0, panels, start_sent, 0)
    lax.fori_loop(0, panels, start_local, 0)
    local_coup.start()

    tab[...] = jnp.zeros_like(tab)
    tab[0:2, :] = 1.0 / tc_ref[...]
    tab[2:4, :] = amp_ref[...]
    whole = tab[0:4, :]
    high = whole.astype(jnp.bfloat16).astype(jnp.float32)
    middle = (whole - high).astype(jnp.bfloat16).astype(jnp.float32)
    tab[0:4, :] = high
    tab[4:8, :] = middle
    tab[8:12, :] = whole - high - middle
    i = lax.broadcasted_iota(jnp.int32, (rows, rows), 0)
    j = lax.broadcasted_iota(jnp.int32, (rows, rows), 1)
    keep = jnp.where((i // steps == j // steps) & (j <= i), 1.0, 0.0).astype(jnp.bfloat16)
    lower[:, 0:rows] = keep
    lower[:, rows:] = keep

    def prepare(b, _):
        k, lanes = b // CHUNK, pl.ds(pl.multiple_of((b % CHUNK) * width, width), width)
        station = sub_ref[pl.ds(b, 1), :]
        onehot = jnp.where(
            lax.broadcasted_iota(jnp.int32, (groups, width), 0) == station, 1.0, 0.0
        ).astype(jnp.bfloat16)
        parts = jnp.dot(tab[...].astype(jnp.bfloat16), onehot, preferred_element_type=jnp.float32)
        found = parts[0:4] + parts[4:8] + parts[8:12]
        t = lax.broadcasted_iota(jnp.int32, (steps, width), 0).astype(jnp.float32)
        for r in range(2):
            rate = found[r : r + 1]
            decay = jnp.exp(-rate)
            scale = found[2 + r : 3 + r] * (1.0 - decay)
            grow[b, r] = jnp.exp(t * rate)
            fade[b, r] = jnp.exp(-t * rate) * scale
            span[k, scen * r : scen * (r + 1), lanes] = jnp.broadcast_to(
                jnp.exp(-float(steps) * rate), (scen, width)
            )
            once[k, scen * r : scen * (r + 1), lanes] = jnp.broadcast_to(decay, (scen, width))
        return 0

    lax.fori_loop(0, blocks, prepare, 0, unroll=2)

    local_coup.wait()
    lax.fori_loop(0, panels, wait_panels, 0)

    def peer_copy(k):
        return pltpu.make_async_remote_copy(
            src_ref=ends.at[k], dst_ref=peer_ends.at[k],
            send_sem=peer_send.at[k], recv_sem=peer_recv.at[k],
            device_id={"tm": partner}, device_id_type=MESH,
        )

    def chain_copy(k):
        return pltpu.make_async_remote_copy(
            src_ref=chain_out.at[k], dst_ref=chain_in.at[k],
            send_sem=chain_send.at[k], recv_sem=chain_recv.at[k],
            device_id={"tm": me + 2}, device_id_type=MESH,
        )

    def couple(k, _):
        def one(n, _):
            b = k * CHUNK + n
            lanes = pl.ds(pl.multiple_of(n * width, width), width)
            picked = jnp.concatenate(
                [
                    vbuf[pat_ref[b, slot]].reshape(rows, panel)
                    for slot in range(slots)
                ],
                axis=1,
            )
            current = jnp.dot(picked, cbuf[b], preferred_element_type=jnp.float32)
            heat = jnp.abs(current).astype(jnp.bfloat16)
            hbuf[b] = heat
            heat = heat.astype(jnp.float32).reshape(scen, steps, width)
            for r in range(2):
                top = grow[b, r]
                total = jnp.sum(heat * top[None], axis=1)
                ends[k, scen * r : scen * (r + 1), lanes] = total / top[steps - 1 : steps]
            return 0

        lax.fori_loop(0, CHUNK, one, 0, unroll=2)
        peer_copy(k).start()
        return 0

    lax.fori_loop(0, chunks, couple, 0)

    @pl.when(jnp.logical_not(has_prev))
    def _():
        chain_in[...] = jnp.zeros_like(chain_in)

    def finish(k, _):
        peer_copy(k).wait_recv()

        @pl.when(has_prev)
        def _():
            chain_copy(k).wait_recv()

        first = jnp.where(odd == 0, ends[k], peer_ends[k])
        second = jnp.where(odd == 0, peer_ends[k], ends[k])
        over = span[k]
        came = chain_in[k]
        middle = over * came + first

        @pl.when(has_next)
        def _():
            chain_out[k] = over * middle + second
            chain_copy(k).start()

        carry[...] = once[k] * jnp.where(odd == 0, came, middle)

        def one(n, _):
            b = k * CHUNK + n
            lanes = pl.ds(pl.multiple_of(n * width, width), width)
            heat = hbuf[b].astype(jnp.float32).reshape(scen, steps, width)
            highs, lows = [], []
            for r in range(2):
                grown = (heat * grow[b, r][None]).reshape(rows, width)
                high = grown.astype(jnp.bfloat16)
                highs.append(high)
                lows.append((grown - high.astype(jnp.float32)).astype(jnp.bfloat16))
            right = jnp.concatenate(
                [jnp.concatenate(highs, axis=1), jnp.concatenate(lows, axis=1)], axis=0
            )
            summed = jnp.dot(lower[...], right, preferred_element_type=jnp.float32)
            total = None
            for r in range(2):
                part = summed[:, r * width : (r + 1) * width].reshape(scen, steps, width)
                begun = carry[scen * r : scen * (r + 1), lanes]
                term = fade[b, r][None] * (part + begun[:, None, :])
                total = term if total is None else total + term
            obuf[k, :, :, lanes] = total.astype(jnp.bfloat16)
            return 0

        lax.fori_loop(0, CHUNK, one, 0, unroll=2)
        out_copy(k).start()
        return 0

    def out_copy(k):
        span_lanes = CHUNK * width
        return pltpu.make_async_copy(
            obuf.at[k],
            out_ref.at[:, :, pl.ds(pl.multiple_of(k * span_lanes, span_lanes), span_lanes)],
            out_sem.at[k],
        )

    lax.fori_loop(0, chunks, finish, 0)

    def drain(k, _):
        out_copy(k).wait()
        peer_copy(k).wait_send()

        @pl.when(has_next)
        def _():
            chain_copy(k).wait_send()

        return 0

    lax.fori_loop(0, chunks, drain, 0)


def body(pairs, voltages, coupling, pattern, substation, time_const, amplitude):
    scen, steps, lines = voltages.shape
    blocks, slots, panel, width = coupling.shape
    chunks = blocks // CHUNK
    lanes = CHUNK * width
    rows = scen * steps
    state = (chunks, 2 * scen, lanes)
    vmem = pl.BlockSpec(memory_space=pltpu.VMEM)
    hbm = pl.BlockSpec(memory_space=pl.ANY)
    dma = pltpu.SemaphoreType.DMA
    return pl.pallas_call(
        functools.partial(kernel, pairs),
        out_shape=jax.ShapeDtypeStruct((scen, steps, blocks * width), jnp.bfloat16),
        in_specs=[hbm, hbm, pl.BlockSpec(memory_space=pltpu.SMEM), vmem, vmem, vmem],
        out_specs=hbm,
        scratch_shapes=[
            pltpu.VMEM((2 * lines // panel, scen, steps, panel), jnp.bfloat16),
            pltpu.VMEM((blocks, slots * panel, width), jnp.bfloat16),
            pltpu.VMEM((blocks, rows, width), jnp.bfloat16),
            pltpu.VMEM((blocks, 2, steps, width), jnp.float32),
            pltpu.VMEM((blocks, 2, steps, width), jnp.float32),
            pltpu.VMEM(state, jnp.float32),
            pltpu.VMEM(state, jnp.float32),
            pltpu.VMEM(state, jnp.float32),
            pltpu.VMEM(state, jnp.float32),
            pltpu.VMEM(state[1:], jnp.float32),
            pltpu.VMEM(state, jnp.float32),
            pltpu.VMEM(state, jnp.float32),
            pltpu.VMEM((16, time_const.shape[0]), jnp.float32),
            pltpu.VMEM((rows, 2 * rows), jnp.bfloat16),
            pltpu.VMEM((chunks, scen, steps, lanes), jnp.bfloat16),
            dma((lines // panel,)),
            dma,
            dma((chunks,)),
            dma((lines // panel,)),
            dma((lines // panel,)),
            dma((chunks,)),
            dma((chunks,)),
            dma((chunks,)),
            dma((chunks,)),
        ],
        compiler_params=pltpu.CompilerParams(
            collective_id=0, has_side_effects=True, vmem_limit_bytes=48 * 1024 * 1024
        ),
    )(
        voltages,
        coupling.reshape(blocks, slots * panel, width),
        pattern,
        substation.reshape(blocks, width),
        time_const.T,
        amplitude.T,
    )


def solution(mesh):
    in_specs = (
        P("scen", "tm", "xfmr"),
        P("xfmr", None, None, None),
        P("xfmr", None),
        P("xfmr"),
        P(),
        P(),
    )
    out_specs = P("scen", "tm", "xfmr")
    return jax.shard_map(
        functools.partial(body, mesh.shape["tm"] // 2),
        mesh=mesh, in_specs=in_specs, out_specs=out_specs, check_vma=False,
    )
```

```python
import functools
import jax
import jax.numpy as jnp
from jax import lax
from jax.experimental import pallas as pl
from jax.experimental.pallas import tpu as pltpu
from jax.sharding import PartitionSpec as P

MESH = pl.DeviceIdType.MESH
CHUNK = 4
UNROLL_A = 4
UNROLL_B = 4
UNROLL_C = 4
UNROLL_P = 4
LAG = 8
LAG_PAIR = 4


def kernel(
    pairs, volt_ref, coup_ref, pat_hbm, sub_hbm, tc_hbm, amp_hbm, out_ref,
    pat_ref, sub_ref, tc_ref, amp_ref, vbuf, cbuf, hbuf, grow, fade, ends, peer_ends, chain_in, chain_out, carry, span, once,
    tab, lower, lbuf, obuf,
    small_sem, volt_sem, coup_sem, out_sem, gather_send, gather_recv, peer_send, peer_recv, chain_send, chain_recv,
):
    scen, steps, lines = volt_ref.shape
    blocks, depth, width = coup_ref.shape
    rows = scen * steps
    groups = tc_ref.shape[1]
    slots = pat_ref.shape[0]
    panel = depth // slots
    chunks = blocks // CHUNK
    core = lax.axis_index("xfmr")
    me = lax.axis_index("tm")
    pair = me // 2
    odd = me % 2
    partner = me + 1 - 2 * odd
    has_prev = pair > 0
    has_next = pair < pairs - 1

    barrier = pltpu.get_barrier_semaphore()
    pl.semaphore_signal(barrier, inc=1, device_id={"xfmr": 1 - core}, device_id_type=MESH)
    pl.semaphore_signal(barrier, inc=1, device_id={"tm": partner}, device_id_type=MESH)

    @pl.when(has_prev)
    def _():
        pl.semaphore_signal(barrier, inc=1, device_id={"tm": me - 2}, device_id_type=MESH)

    @pl.when(has_next)
    def _():
        pl.semaphore_signal(barrier, inc=1, device_id={"tm": me + 2}, device_id_type=MESH)

    panels = lines // panel

    def local_panel(n):
        return pltpu.make_async_copy(
            volt_ref.at[:, :, pl.ds(pl.multiple_of(n * panel, panel), panel)],
            vbuf.at[core * panels + n],
            volt_sem.at[n],
        )

    def sent_panel(n):
        return pltpu.make_async_remote_copy(
            src_ref=volt_ref.at[:, :, pl.ds(pl.multiple_of(n * panel, panel), panel)],
            dst_ref=vbuf.at[core * panels + n],
            send_sem=gather_send.at[n],
            recv_sem=gather_recv.at[n],
            device_id={"xfmr": 1 - core},
            device_id_type=MESH,
        )

    def start_local(n, _):
        local_panel(n).start()
        return 0

    def start_sent(n, _):
        sent_panel(n).start()
        return 0

    def wait_panels(n, _):
        local_panel(n).wait()
        sent_panel(n).wait()
        return 0

    smalls = [
        pltpu.make_async_copy(source, target, small_sem.at[n])
        for n, (source, target) in enumerate(
            ((tc_hbm, tc_ref), (amp_hbm, amp_ref), (sub_hbm, sub_ref), (pat_hbm, pat_ref))
        )
    ]
    for copy in smalls:
        copy.start()
    local_coup = pltpu.make_async_copy(coup_ref, cbuf, coup_sem)
    local_coup.start()
    lax.fori_loop(0, panels, start_local, 0)
    pl.semaphore_wait(barrier, 2 + has_prev.astype(jnp.int32) + has_next.astype(jnp.int32))
    lax.fori_loop(0, panels, start_sent, 0)

    for copy in smalls:
        copy.wait()

    tab[...] = jnp.zeros_like(tab)
    tab[0:2, :] = 1.0 / tc_ref[...]
    tab[2:4, :] = amp_ref[...]
    whole = tab[0:4, :]
    high = whole.astype(jnp.bfloat16).astype(jnp.float32)
    middle = (whole - high).astype(jnp.bfloat16).astype(jnp.float32)
    tab[0:4, :] = high
    tab[4:8, :] = middle
    tab[8:12, :] = whole - high - middle
    i = lax.broadcasted_iota(jnp.int32, lower.shape, 0)
    j = lax.broadcasted_iota(jnp.int32, lower.shape, 1)
    keep = (i // steps == j // (2 * steps)) & (j % steps <= i % steps)
    lower[...] = jnp.where(keep, 1.0, 0.0).astype(jnp.bfloat16)

    def prepare(b, _):
        k, lanes = b // CHUNK, pl.ds(pl.multiple_of((b % CHUNK) * width, width), width)
        station = sub_ref[pl.ds(b, 1), :]
        onehot = jnp.where(
            lax.broadcasted_iota(jnp.int32, (groups, width), 0) == station, 1.0, 0.0
        ).astype(jnp.bfloat16)
        parts = jnp.dot(tab[...].astype(jnp.bfloat16), onehot, preferred_element_type=jnp.float32)
        found = parts[0:4] + parts[4:8] + parts[8:12]
        t = lax.broadcasted_iota(jnp.int32, (steps, width), 0).astype(jnp.float32)
        for r in range(2):
            rate = found[r : r + 1]
            decay = jnp.exp(-rate)
            scale = found[2 + r : 3 + r] * (1.0 - decay)
            grow[b, r] = jnp.exp(t * rate)
            fade[b, r] = jnp.exp(-t * rate) * scale
            span[k, scen * r : scen * (r + 1), lanes] = jnp.broadcast_to(
                jnp.exp(-float(steps) * rate), (scen, width)
            )
            once[k, scen * r : scen * (r + 1), lanes] = jnp.broadcast_to(decay, (scen, width))
        return 0

    lax.fori_loop(0, blocks, prepare, 0, unroll=UNROLL_P)

    local_coup.wait()
    lax.fori_loop(0, panels, wait_panels, 0)

    def peer_copy(k):
        return pltpu.make_async_remote_copy(
            src_ref=ends.at[k], dst_ref=peer_ends.at[k],
            send_sem=peer_send.at[k], recv_sem=peer_recv.at[k],
            device_id={"tm": partner}, device_id_type=MESH,
        )

    def chain_copy(k):
        return pltpu.make_async_remote_copy(
            src_ref=chain_out.at[k], dst_ref=chain_in.at[k],
            send_sem=chain_send.at[k], recv_sem=chain_recv.at[k],
            device_id={"tm": me + 2}, device_id_type=MESH,
        )

    def couple(k):
        def one(n, _):
            b = k * CHUNK + n
            lanes = pl.ds(pl.multiple_of(n * width, width), width)
            picked = jnp.concatenate(
                [
                    vbuf[pat_ref[slot, b]].reshape(rows, panel)
                    for slot in range(slots)
                ],
                axis=1,
            )
            current = jnp.dot(picked, cbuf[b], preferred_element_type=jnp.float32)
            heat = jnp.abs(current).astype(jnp.bfloat16)
            hbuf[b] = heat
            heat = heat.astype(jnp.float32).reshape(scen, steps, width)
            for r in range(2):
                top = grow[b, r]
                total = jnp.sum(heat * top[None], axis=1)
                ends[k, scen * r : scen * (r + 1), lanes] = total / top[steps - 1 : steps]
            return 0

        lax.fori_loop(0, CHUNK, one, 0, unroll=UNROLL_A)
        peer_copy(k).start()

    @pl.when(jnp.logical_not(has_prev))
    def _():
        chain_in[...] = jnp.zeros_like(chain_in)

    def advance(k):
        peer_copy(k).wait_recv()

        @pl.when(has_prev)
        def _():
            chain_copy(k).wait_recv()

        first = jnp.where(odd == 0, ends[k], peer_ends[k])
        second = jnp.where(odd == 0, peer_ends[k], ends[k])
        over = span[k]
        came = chain_in[k]
        middle = over * came + first

        @pl.when(has_next)
        def _():
            chain_out[k] = over * middle + second
            chain_copy(k).start()

        carry[k] = once[k] * jnp.where(odd == 0, came, middle)

    def out_copy(k):
        span_lanes = CHUNK * width
        return pltpu.make_async_copy(
            obuf.at[k],
            out_ref.at[:, :, pl.ds(pl.multiple_of(k * span_lanes, span_lanes), span_lanes)],
            out_sem.at[k],
        )

    def convolve(k):
        def one(n, _):
            b = k * CHUNK + n
            lanes = pl.ds(pl.multiple_of(n * width, width), width)
            for s in range(0, scen, 2):
                columns = []
                for r in range(2):
                    parts = []
                    for u in (s, s + 1):
                        heat = hbuf[b, u * steps : (u + 1) * steps].astype(jnp.float32)
                        grown = heat * grow[b, r]
                        high = grown.astype(jnp.bfloat16)
                        parts.append(high)
                        parts.append((grown - high.astype(jnp.float32)).astype(jnp.bfloat16))
                    columns.append(jnp.concatenate(parts, axis=0))
                summed = jnp.dot(
                    lower[...], jnp.concatenate(columns, axis=1), preferred_element_type=jnp.float32
                )
                for v in range(2):
                    total = None
                    for r in range(2):
                        part = summed[v * steps : (v + 1) * steps, r * width : (r + 1) * width]
                        term = fade[b, r] * part
                        total = term if total is None else total + term
                    lbuf[b, s + v] = total
            return 0

        lax.fori_loop(0, CHUNK, one, 0, unroll=UNROLL_B)

    def combine(k):
        def one(n, _):
            b = k * CHUNK + n
            lanes = pl.ds(pl.multiple_of(n * width, width), width)
            for s in range(scen):
                total = lbuf[b, s]
                for r in range(2):
                    row = scen * r + s
                    total = total + fade[b, r] * carry[k, row : row + 1, lanes]
                obuf[k, s, :, lanes] = total.astype(jnp.bfloat16)
            return 0

        lax.fori_loop(0, CHUNK, one, 0, unroll=UNROLL_C)
        out_copy(k).start()

    lag = jnp.minimum(LAG + LAG_PAIR * pair, 2 * chunks)
    delay = jnp.maximum(lag, chunks)

    def step(n, _):
        late = n - lag
        last = n - delay

        @pl.when((late >= 0) & (late < chunks))
        def _():
            advance(late)

        @pl.when(n < chunks)
        def _():
            couple(n)

        @pl.when((n >= chunks) & (n < 2 * chunks))
        def _():
            convolve(n - chunks)

        @pl.when(last >= 0)
        def _():
            combine(last)

        return 0

    lax.fori_loop(0, chunks + delay, step, 0)

    def drain(k, _):
        out_copy(k).wait()
        peer_copy(k).wait_send()

        @pl.when(has_next)
        def _():
            chain_copy(k).wait_send()

        return 0

    lax.fori_loop(0, chunks, drain, 0)


def body(pairs, voltages, coupling, pattern, substation, time_const, amplitude):
    scen, steps, lines = voltages.shape
    blocks, slots, panel, width = coupling.shape
    chunks = blocks // CHUNK
    lanes = CHUNK * width
    rows = scen * steps
    state = (chunks, 2 * scen, lanes)
    hbm = pl.BlockSpec(memory_space=pltpu.HBM)
    dma = pltpu.SemaphoreType.DMA
    return pl.pallas_call(
        functools.partial(kernel, pairs),
        out_shape=pltpu.VMEM((scen, steps, blocks * width), jnp.bfloat16),
        in_specs=[hbm] * 6,
        out_specs=pl.BlockSpec(memory_space=pl.ANY),
        scratch_shapes=[
            pltpu.SMEM((slots, blocks), jnp.int32),
            pltpu.VMEM((blocks, width), jnp.int32),
            pltpu.VMEM(time_const.shape[::-1], jnp.float32),
            pltpu.VMEM(amplitude.shape[::-1], jnp.float32),
            pltpu.VMEM((2 * lines // panel, scen, steps, panel), jnp.bfloat16),
            pltpu.VMEM((blocks, slots * panel, width), jnp.bfloat16),
            pltpu.VMEM((blocks, rows, width), jnp.bfloat16),
            pltpu.VMEM((blocks, 2, steps, width), jnp.float32),
            pltpu.VMEM((blocks, 2, steps, width), jnp.float32),
            pltpu.VMEM(state, jnp.float32),
            pltpu.VMEM(state, jnp.float32),
            pltpu.VMEM(state, jnp.float32),
            pltpu.VMEM(state, jnp.float32),
            pltpu.VMEM(state, jnp.float32),
            pltpu.VMEM(state, jnp.float32),
            pltpu.VMEM(state, jnp.float32),
            pltpu.VMEM((16, time_const.shape[0]), jnp.float32),
            pltpu.VMEM((2 * steps, 4 * steps), jnp.bfloat16),
            pltpu.VMEM((blocks, scen, steps, width), jnp.float32),
            pltpu.VMEM((chunks, scen, steps, lanes), jnp.bfloat16),
            dma((4,)),
            dma((lines // panel,)),
            dma,
            dma((chunks,)),
            dma((lines // panel,)),
            dma((lines // panel,)),
            dma((chunks,)),
            dma((chunks,)),
            dma((chunks,)),
            dma((chunks,)),
        ],
        compiler_params=pltpu.CompilerParams(
            collective_id=0, has_side_effects=True, vmem_limit_bytes=60 * 1024 * 1024
        ),
    )(
        voltages,
        coupling.reshape(blocks, slots * panel, width),
        pattern.T,
        substation.reshape(blocks, width),
        time_const.T,
        amplitude.T,
    )


def solution(mesh):
    in_specs = (
        P("scen", "tm", "xfmr"),
        P("xfmr", None, None, None),
        P("xfmr", None),
        P("xfmr"),
        P(),
        P(),
    )
    out_specs = P("scen", "tm", "xfmr")
    return jax.shard_map(
        functools.partial(body, mesh.shape["tm"] // 2),
        mesh=mesh, in_specs=in_specs, out_specs=out_specs, check_vma=False,
    )
```

```python
import functools
import jax
import jax.numpy as jnp
from jax import lax
from jax.experimental import pallas as pl
from jax.experimental.pallas import tpu as pltpu
from jax.sharding import PartitionSpec as P

MESH = pl.DeviceIdType.MESH
CHUNK = 4
UNROLL_A = 4
UNROLL_B = 4
UNROLL_C = 4
UNROLL_P = 4
LAG = 8
LAG_PAIR = 4


def kernel(
    pairs, volt_ref, coup_ref, pat_hbm, sub_hbm, tc_hbm, amp_hbm, out_ref,
    pat_ref, sub_ref, tc_ref, amp_ref, vbuf, cbuf, hbuf, grow, fade, ends, peer_ends, chain_in, chain_out, carry, span, once,
    tab, lower, lbuf,
    small_sem, volt_sem, coup_sem, gather_send, gather_recv, peer_send, peer_recv, chain_send, chain_recv,
):
    scen, steps, lines = volt_ref.shape
    blocks, depth, width = coup_ref.shape
    rows = scen * steps
    groups = tc_ref.shape[1]
    slots = pat_ref.shape[0]
    panel = depth // slots
    chunks = blocks // CHUNK
    core = lax.axis_index("xfmr")
    me = lax.axis_index("tm")
    pair = me // 2
    odd = me % 2
    partner = me + 1 - 2 * odd
    has_prev = pair > 0
    has_next = pair < pairs - 1

    barrier = pltpu.get_barrier_semaphore()
    pl.semaphore_signal(barrier, inc=1, device_id={"xfmr": 1 - core}, device_id_type=MESH)
    pl.semaphore_signal(barrier, inc=1, device_id={"tm": partner}, device_id_type=MESH)

    @pl.when(has_prev)
    def _():
        pl.semaphore_signal(barrier, inc=1, device_id={"tm": me - 2}, device_id_type=MESH)

    @pl.when(has_next)
    def _():
        pl.semaphore_signal(barrier, inc=1, device_id={"tm": me + 2}, device_id_type=MESH)

    panels = lines // panel

    def local_panel(n):
        return pltpu.make_async_copy(
            volt_ref.at[:, :, pl.ds(pl.multiple_of(n * panel, panel), panel)],
            vbuf.at[core * panels + n],
            volt_sem.at[n],
        )

    def sent_panel(n):
        return pltpu.make_async_remote_copy(
            src_ref=volt_ref.at[:, :, pl.ds(pl.multiple_of(n * panel, panel), panel)],
            dst_ref=vbuf.at[core * panels + n],
            send_sem=gather_send.at[n],
            recv_sem=gather_recv.at[n],
            device_id={"xfmr": 1 - core},
            device_id_type=MESH,
        )

    def start_local(n, _):
        local_panel(n).start()
        return 0

    def start_sent(n, _):
        sent_panel(n).start()
        return 0

    def wait_panels(n, _):
        local_panel(n).wait()
        sent_panel(n).wait()
        return 0

    smalls = [
        pltpu.make_async_copy(source, target, small_sem.at[n])
        for n, (source, target) in enumerate(
            ((tc_hbm, tc_ref), (amp_hbm, amp_ref), (sub_hbm, sub_ref), (pat_hbm, pat_ref))
        )
    ]
    for copy in smalls:
        copy.start()
    local_coup = pltpu.make_async_copy(coup_ref, cbuf, coup_sem)
    local_coup.start()
    lax.fori_loop(0, panels, start_local, 0)
    pl.semaphore_wait(barrier, 2 + has_prev.astype(jnp.int32) + has_next.astype(jnp.int32))
    lax.fori_loop(0, panels, start_sent, 0)

    for copy in smalls:
        copy.wait()

    tab[...] = jnp.zeros_like(tab)
    tab[0:2, :] = 1.0 / tc_ref[...]
    tab[2:4, :] = amp_ref[...]
    whole = tab[0:4, :]
    high = whole.astype(jnp.bfloat16).astype(jnp.float32)
    middle = (whole - high).astype(jnp.bfloat16).astype(jnp.float32)
    tab[0:4, :] = high
    tab[4:8, :] = middle
    tab[8:12, :] = whole - high - middle
    i = lax.broadcasted_iota(jnp.int32, lower.shape, 0)
    j = lax.broadcasted_iota(jnp.int32, lower.shape, 1)
    keep = (i // steps == j // (2 * steps)) & (j % steps <= i % steps)
    lower[...] = jnp.where(keep, 1.0, 0.0).astype(jnp.bfloat16)

    def prepare(b, _):
        k, lanes = b // CHUNK, pl.ds(pl.multiple_of((b % CHUNK) * width, width), width)
        station = sub_ref[pl.ds(b, 1), :]
        onehot = jnp.where(
            lax.broadcasted_iota(jnp.int32, (groups, width), 0) == station, 1.0, 0.0
        ).astype(jnp.bfloat16)
        parts = jnp.dot(tab[...].astype(jnp.bfloat16), onehot, preferred_element_type=jnp.float32)
        found = parts[0:4] + parts[4:8] + parts[8:12]
        t = lax.broadcasted_iota(jnp.int32, (steps, width), 0).astype(jnp.float32)
        for r in range(2):
            rate = found[r : r + 1]
            decay = jnp.exp(-rate)
            scale = found[2 + r : 3 + r] * (1.0 - decay)
            grow[b, r] = jnp.exp(t * rate)
            fade[b, r] = jnp.exp(-t * rate) * scale
            span[k, scen * r : scen * (r + 1), lanes] = jnp.broadcast_to(
                jnp.exp(-float(steps) * rate), (scen, width)
            )
            once[k, scen * r : scen * (r + 1), lanes] = jnp.broadcast_to(decay, (scen, width))
        return 0

    lax.fori_loop(0, blocks, prepare, 0, unroll=UNROLL_P)

    local_coup.wait()
    lax.fori_loop(0, panels, wait_panels, 0)

    def peer_copy(k):
        return pltpu.make_async_remote_copy(
            src_ref=ends.at[k], dst_ref=peer_ends.at[k],
            send_sem=peer_send.at[k], recv_sem=peer_recv.at[k],
            device_id={"tm": partner}, device_id_type=MESH,
        )

    def chain_copy(k):
        return pltpu.make_async_remote_copy(
            src_ref=chain_out.at[k], dst_ref=chain_in.at[k],
            send_sem=chain_send.at[k], recv_sem=chain_recv.at[k],
            device_id={"tm": me + 2}, device_id_type=MESH,
        )

    def couple(k):
        def one(n, _):
            b = k * CHUNK + n
            lanes = pl.ds(pl.multiple_of(n * width, width), width)
            picked = jnp.concatenate(
                [
                    vbuf[pat_ref[slot, b]].reshape(rows, panel)
                    for slot in range(slots)
                ],
                axis=1,
            )
            current = jnp.dot(picked, cbuf[b], preferred_element_type=jnp.float32)
            heat = jnp.abs(current).astype(jnp.bfloat16)
            hbuf[b] = heat
            heat = heat.astype(jnp.float32).reshape(scen, steps, width)
            for r in range(2):
                top = grow[b, r]
                total = jnp.sum(heat * top[None], axis=1)
                ends[k, scen * r : scen * (r + 1), lanes] = total / top[steps - 1 : steps]
            return 0

        lax.fori_loop(0, CHUNK, one, 0, unroll=UNROLL_A)
        peer_copy(k).start()

    @pl.when(jnp.logical_not(has_prev))
    def _():
        chain_in[...] = jnp.zeros_like(chain_in)

    def advance(k):
        peer_copy(k).wait_recv()

        @pl.when(has_prev)
        def _():
            chain_copy(k).wait_recv()

        first = jnp.where(odd == 0, ends[k], peer_ends[k])
        second = jnp.where(odd == 0, peer_ends[k], ends[k])
        over = span[k]
        came = chain_in[k]
        middle = over * came + first

        @pl.when(has_next)
        def _():
            chain_out[k] = over * middle + second
            chain_copy(k).start()

        carry[k] = once[k] * jnp.where(odd == 0, came, middle)

    def convolve(k):
        def one(n, _):
            b = k * CHUNK + n
            lanes = pl.ds(pl.multiple_of(n * width, width), width)
            for s in range(0, scen, 2):
                columns = []
                for r in range(2):
                    parts = []
                    for u in (s, s + 1):
                        heat = hbuf[b, u * steps : (u + 1) * steps].astype(jnp.float32)
                        grown = heat * grow[b, r]
                        high = grown.astype(jnp.bfloat16)
                        parts.append(high)
                        parts.append((grown - high.astype(jnp.float32)).astype(jnp.bfloat16))
                    columns.append(jnp.concatenate(parts, axis=0))
                summed = jnp.dot(
                    lower[...], jnp.concatenate(columns, axis=1), preferred_element_type=jnp.float32
                )
                for v in range(2):
                    total = None
                    for r in range(2):
                        part = summed[v * steps : (v + 1) * steps, r * width : (r + 1) * width]
                        term = fade[b, r] * part
                        total = term if total is None else total + term
                    lbuf[b, s + v] = total
            return 0

        lax.fori_loop(0, CHUNK, one, 0, unroll=UNROLL_B)

    def combine(k):
        def one(n, _):
            b = k * CHUNK + n
            lanes = pl.ds(pl.multiple_of(n * width, width), width)
            for s in range(scen):
                total = lbuf[b, s]
                for r in range(2):
                    row = scen * r + s
                    total = total + fade[b, r] * carry[k, row : row + 1, lanes]
                out_ref[s, :, pl.ds(pl.multiple_of(b * width, width), width)] = total.astype(jnp.bfloat16)
            return 0

        lax.fori_loop(0, CHUNK, one, 0, unroll=UNROLL_C)

    lag = jnp.minimum(LAG + LAG_PAIR * pair, 2 * chunks)
    delay = jnp.maximum(lag, chunks)

    def step(n, _):
        late = n - lag
        last = n - delay

        @pl.when((late >= 0) & (late < chunks))
        def _():
            advance(late)

        @pl.when(n < chunks)
        def _():
            couple(n)

        @pl.when((n >= chunks) & (n < 2 * chunks))
        def _():
            convolve(n - chunks)

        @pl.when(last >= 0)
        def _():
            combine(last)

        return 0

    lax.fori_loop(0, chunks + delay, step, 0)

    def drain(k, _):
        peer_copy(k).wait_send()

        @pl.when(has_next)
        def _():
            chain_copy(k).wait_send()

        return 0

    lax.fori_loop(0, chunks, drain, 0)


def body(pairs, voltages, coupling, pattern, substation, time_const, amplitude):
    scen, steps, lines = voltages.shape
    blocks, slots, panel, width = coupling.shape
    chunks = blocks // CHUNK
    lanes = CHUNK * width
    rows = scen * steps
    state = (chunks, 2 * scen, lanes)
    hbm = pl.BlockSpec(memory_space=pltpu.HBM)
    dma = pltpu.SemaphoreType.DMA
    return pl.pallas_call(
        functools.partial(kernel, pairs),
        out_shape=pltpu.VMEM((scen, steps, blocks * width), jnp.bfloat16),
        in_specs=[hbm] * 6,
        out_specs=pl.BlockSpec(memory_space=pltpu.VMEM),
        scratch_shapes=[
            pltpu.SMEM((slots, blocks), jnp.int32),
            pltpu.VMEM((blocks, width), jnp.int32),
            pltpu.VMEM(time_const.shape[::-1], jnp.float32),
            pltpu.VMEM(amplitude.shape[::-1], jnp.float32),
            pltpu.VMEM((2 * lines // panel, scen, steps, panel), jnp.bfloat16),
            pltpu.VMEM((blocks, slots * panel, width), jnp.bfloat16),
            pltpu.VMEM((blocks, rows, width), jnp.bfloat16),
            pltpu.VMEM((blocks, 2, steps, width), jnp.float32),
            pltpu.VMEM((blocks, 2, steps, width), jnp.float32),
            pltpu.VMEM(state, jnp.float32),
            pltpu.VMEM(state, jnp.float32),
            pltpu.VMEM(state, jnp.float32),
            pltpu.VMEM(state, jnp.float32),
            pltpu.VMEM(state, jnp.float32),
            pltpu.VMEM(state, jnp.float32),
            pltpu.VMEM(state, jnp.float32),
            pltpu.VMEM((16, time_const.shape[0]), jnp.float32),
            pltpu.VMEM((2 * steps, 4 * steps), jnp.bfloat16),
            pltpu.VMEM((blocks, scen, steps, width), jnp.float32),
            dma((4,)),
            dma((lines // panel,)),
            dma,
            dma((lines // panel,)),
            dma((lines // panel,)),
            dma((chunks,)),
            dma((chunks,)),
            dma((chunks,)),
            dma((chunks,)),
        ],
        compiler_params=pltpu.CompilerParams(
            collective_id=0, has_side_effects=True, vmem_limit_bytes=60 * 1024 * 1024
        ),
    )(
        voltages,
        coupling.reshape(blocks, slots * panel, width),
        pattern.T,
        substation.reshape(blocks, width),
        time_const.T,
        amplitude.T,
    )


def solution(mesh):
    in_specs = (
        P("scen", "tm", "xfmr"),
        P("xfmr", None, None, None),
        P("xfmr", None),
        P("xfmr"),
        P(),
        P(),
    )
    out_specs = P("scen", "tm", "xfmr")
    return jax.shard_map(
        functools.partial(body, mesh.shape["tm"] // 2),
        mesh=mesh, in_specs=in_specs, out_specs=out_specs, check_vma=False,
    )
```
